128 devices in a mesh: dp: 4 (over y_lo, core), fsdp: 32 (over x, z, y_hi).
Axes of the slice: x: 4, y: 4 (y_hi: 2, y_lo: 2; y = y_hi * 2 + y_lo), z: 4, core: 2. Of those that a mesh axis runs over, the one named last changes fastest.
Arguments:
- normed: bfloat16 [65536, 8192], P(('dp', 'fsdp')), may hold values from -24 to 24
- queries: bfloat16 [65536, 4096], P(('dp', 'fsdp')), may hold values from -96 to 96, as said below
- keys: bfloat16 [65536, 512], P(('dp', 'fsdp')), may hold values from -4.5 to 4.5
- value_weight: bfloat16 [8192, 512], P('fsdp'), may hold values from -0.0625 to 0.0625
- iterate: float32 [8192, 512], P('fsdp'), may hold values from -6 to 6
- residual: float32 [8192, 512], P('fsdp'), may hold values from -6 to 6
- direction: float32 [8192, 512], P('fsdp'), may hold values from -6 to 6
- damping: float32 [1], replicated, may hold values from 0.05 to 0.5
Outputs:
- new_iterate: float32 [8192, 512], P('fsdp')
- new_residual: float32 [8192, 512], P('fsdp')
- new_direction: float32 [8192, 512], P('fsdp')
The draws below stay inside these ranges and needn't reach their ends.
Inputs may be any that keep to these rules, and one draw needn't show every extreme that they name: `queries`: queries are of order one except for a few rows, which may be large multiples of an earlier key of their key-value head.
All inputs are finite; a program needn't handle non-finite values.
Results may differ from the reference program's by a relative error of at most 0.0043.
Values may be sent and summed in bfloat16 or wider, within the bound.
No kernel may reach another device: no remote copies, remote signals or barrier semaphores. Data moves between devices by JAX's collectives and lax.ppermute only.
A program may use at most 192 MiB of HBM per device.

```python
import math
import jax
import jax.numpy as jnp
from jax import lax

D = 8192
HD = 128
HK = 4
HQ = 32
LEN = 512
TOKENS = 65536


def pair_draw(key):
    keys_all = jnp.clip(jax.random.normal(jax.random.fold_in(key, 11), (TOKENS, HK * HD), jnp.float32), -4.5, 4.5)
    queries_all = jnp.clip(jax.random.normal(jax.random.fold_in(key, 12), (TOKENS, HQ * HD), jnp.float32), -4.5, 4.5)
    return (queries_all, keys_all)


def draw_queries(key, part):
    return pair_draw(key)[0].astype(jnp.bfloat16)


def draw_keys(key, part):
    return pair_draw(key)[1].astype(jnp.bfloat16)


def raised(array, own_key, source, target, blocks, factor):
    def block_of(dim):
        return (jnp.arange(array.shape[dim]) // (array.shape[dim] // blocks)).reshape((-1,) + (1,) * (array.ndim - 1 - dim))

    near = jax.random.permutation(own_key, blocks)[block_of(target)]
    other_side = (block_of(target) + blocks // 2) % blocks
    return jnp.where((block_of(source) == near) | (block_of(source) == other_side), factor * array, array)


def shard_levels(own_key, extent, cuts, low, top_value):
    loudness, own = 1.0, jax.random.fold_in(own_key, 6)
    for axis_at, shards_of in cuts:
        steps = jnp.exp(jax.random.uniform(jax.random.fold_in(own, axis_at), (shards_of,), jnp.float32, low / len(cuts), top_value / len(cuts)))
        loudness = loudness * jnp.repeat(steps, extent[axis_at] // shards_of).reshape([-1 if axis == axis_at else 1 for axis in range(len(extent))])
    return loudness


def centred(own_key, shape, scale, reach, cuts=(), kind=jnp.bfloat16):
    gain = shard_levels(own_key, shape, cuts, -0.22, 0.18) if cuts else 1.0
    entries = jax.random.normal(own_key, shape, jnp.float32) * scale * gain
    return jnp.minimum(jnp.maximum(entries, -reach), reach).astype(kind)


def gaussian_with(own_key, extent, deviation, bound, pieces, heavy, held_as=jnp.bfloat16):
    array = deviation * jax.random.normal(own_key, extent, jnp.float32)
    if pieces:
        array = array * shard_levels(own_key, extent, pieces, -0.22, 0.18)
    return jnp.clip(raised(array, jax.random.fold_in(own_key, 3), *heavy), -bound, bound).astype(held_as)


def setup_inputs(seed: int = 0) -> dict:
    key_of = jax.random.split(jax.random.key(seed), 9)
    return {
        "normed": gaussian_with(key_of[0], (TOKENS, D), 1.0, 24.0, ((0, 128),), (0, 1, 128, 5.5)),
        "queries": draw_queries(jax.random.fold_in(key_of[8], 71), 0),
        "keys": draw_keys(jax.random.fold_in(key_of[8], 71), 0),
        "value_weight": centred(key_of[3], (D, HK * HD), D ** -0.5, 0.0625, ((0, 32),)),
        "iterate": centred(key_of[4], (D, HK * HD), 1.0, 6.0, ((0, 32),), jnp.float32),
        "residual": centred(key_of[5], (D, HK * HD), 1.0, 6.0, ((0, 32),), jnp.float32),
        "direction": centred(key_of[6], (D, HK * HD), 1.0, 6.0, ((0, 32),), jnp.float32),
        "damping": jnp.clip(jax.random.uniform(key_of[7], (1,), jnp.float32, 0.05, 0.5), 0.05, 0.5),
    }


EPSILON = 1e-05

def pull_back(query_rows, key_rows, value_rows, tangent_rows, head_size):
    seq_len = query_rows.shape[0]
    kv_heads = key_rows.shape[1] // head_size
    per_group = query_rows.shape[1] // key_rows.shape[1]
    queries_split = query_rows.astype(jnp.float32).reshape(seq_len, kv_heads, per_group, head_size)
    keys_split = key_rows.astype(jnp.float32).reshape(seq_len, kv_heads, head_size)
    scores = jnp.einsum('tgjd,sgd->gjts', queries_split, keys_split) / math.sqrt(head_size)
    positions = lax.iota(jnp.int32, seq_len)
    causal = positions[:, None] >= positions[None, :]
    scores = jnp.where(causal, scores, -jnp.inf)
    highest = lax.optimization_barrier(jnp.max(scores, axis=-1, keepdims=True))
    exps = jnp.exp(scores - highest)
    weights_soft = (exps / lax.optimization_barrier(jnp.sum(exps, axis=-1, keepdims=True))).astype(jnp.bfloat16).astype(jnp.float32)
    values_split = value_rows.astype(jnp.float32).reshape(seq_len, kv_heads, head_size)
    tangent_split = tangent_rows.astype(jnp.float32).reshape(seq_len, kv_heads, head_size)
    outputs = jnp.einsum('gjts,sgd->tgjd', weights_soft, values_split)
    tangents = jnp.einsum('gjts,sgd->tgjd', weights_soft, tangent_split)
    inverse = lax.rsqrt(lax.optimization_barrier(jnp.mean(outputs * outputs, axis=-1, keepdims=True)) + EPSILON)
    normal_out = outputs * inverse

    def jacobian(vector):
        return (vector - normal_out * lax.optimization_barrier(jnp.mean(normal_out * vector, axis=-1, keepdims=True))) * inverse
    wback = jacobian(jacobian(tangents)).astype(jnp.bfloat16).astype(jnp.float32)
    pulled = jnp.einsum('gjts,tgjd->sgd', weights_soft, wback)
    return pulled.reshape(seq_len, kv_heads * head_size).astype(jnp.bfloat16)

def reference(normed, queries, keys, value_weight, iterate, residual, direction, damping):
    kv_width = HK * HD
    dir_half = direction.astype(jnp.bfloat16)
    joined = jnp.concatenate([value_weight, dir_half], axis=1)

    def advance(running, index):
        offset = (index * LEN).astype(jnp.int32)
        rows_x = lax.dynamic_slice_in_dim(normed, offset, LEN, 0)
        rows_q = lax.dynamic_slice_in_dim(queries, offset, LEN, 0)
        rows_k = lax.dynamic_slice_in_dim(keys, offset, LEN, 0)
        projected = jnp.dot(rows_x, joined, preferred_element_type=jnp.float32).astype(jnp.bfloat16)
        pulled = pull_back(rows_q, rows_k, projected[:, :kv_width], projected[:, kv_width:], HD)
        running = running + jnp.dot(rows_x.T, pulled, preferred_element_type=jnp.float32)
        return (running, None)
    summed, _ = lax.scan(advance, jnp.zeros((D, kv_width), jnp.float32), jnp.arange(TOKENS // LEN, dtype=jnp.int32))
    hessian_dir = summed / TOKENS + damping[0] * direction
    old_sq = jnp.sum(residual * residual)
    curv_sum = jnp.sum(direction * hessian_dir)
    step_size = old_sq / curv_sum
    new_iterate = iterate + step_size * direction
    new_residual = residual - step_size * hessian_dir
    new_sq = jnp.sum(new_residual * new_residual)
    new_direction = new_residual + new_sq / old_sq * direction
    return (new_iterate, new_residual, new_direction)
```

```python
import math

import jax
import jax.numpy as jnp
from jax import lax
from jax.experimental import pallas as pl
from jax.experimental.pallas import tpu as pltpu
from jax.sharding import Mesh, PartitionSpec as P

HD = 128
EPSILON = 1e-05
BF = jnp.bfloat16
F32 = jnp.float32
LEN = 512
HALF = 256
WIDE = 256
PER = 8
VMEM = 56 * 1024 * 1024
NT = (((1,), (1,)), ((), ()))
Y_SWAP = [(0, 3), (3, 0), (2, 1), (1, 2)]


def _params(n):
    return pltpu.CompilerParams(
        dimension_semantics=("arbitrary",) * n, vmem_limit_bytes=VMEM
    )


Q_STEP = 4


def _probs_kernel(off, q_ref, k_ref, o_ref):
    del off
    factor = math.log2(math.e) / math.sqrt(HD)
    rows = lax.broadcasted_iota(jnp.int32, (HALF, HALF), 0)
    cols = lax.broadcasted_iota(jnp.int32, (HALF, HALF), 1)
    seen = rows <= cols
    for j in range(Q_STEP):
        q = q_ref[:, j * HD : (j + 1) * HD]
        diag = lax.dot_general(k_ref[:HALF], q[:HALF], NT, preferred_element_type=F32)
        diag = jnp.where(seen, diag, -jnp.inf)
        top = jnp.max(diag, axis=0, keepdims=True)
        e = jnp.exp2((diag - top) * factor)
        o_ref[j, :HALF] = (e * (1.0 / jnp.sum(e, axis=0, keepdims=True))).astype(BF)
        low = lax.dot_general(k_ref[:HALF], q[HALF:], NT, preferred_element_type=F32)
        diag = lax.dot_general(k_ref[HALF:], q[HALF:], NT, preferred_element_type=F32)
        diag = jnp.where(seen, diag, -jnp.inf)
        top = jnp.maximum(
            jnp.max(low, axis=0, keepdims=True), jnp.max(diag, axis=0, keepdims=True)
        )
        e = jnp.exp2((low - top) * factor)
        f = jnp.exp2((diag - top) * factor)
        inv = 1.0 / (
            jnp.sum(e, axis=0, keepdims=True) + jnp.sum(f, axis=0, keepdims=True)
        )
        o_ref[j, HALF : 2 * HALF] = (e * inv).astype(BF)
        o_ref[j, 2 * HALF :] = (f * inv).astype(BF)


def probs_of(offset, queries, keys):
    heads = 2 * PER
    steps = heads // Q_STEP
    per = steps // 2
    return pl.pallas_call(
        _probs_kernel,
        grid_spec=pltpu.PrefetchScalarGridSpec(
            num_scalar_prefetch=1,
            grid=(steps,),
            in_specs=[
                pl.BlockSpec((LEN, Q_STEP * HD), lambda i, o: (0, o[0] * steps + i)),
                pl.BlockSpec((LEN, HD), lambda i, o: (0, o[0] * 2 + i // per)),
            ],
            out_specs=pl.BlockSpec((Q_STEP, 3 * HALF, HALF), lambda i, o: (i, 0, 0)),
        ),
        out_shape=jax.ShapeDtypeStruct((heads, 3 * HALF, HALF), BF),
        compiler_params=_params(1),
        cost_estimate=pl.CostEstimate(
            flops=heads * 3 * HALF * HALF * HD * 2,
            bytes_accessed=heads * 3 * HALF * HALF * 2 + LEN * heads * HD * 2,
            transcendentals=heads * 3 * HALF * HALF,
        ),
    )(offset, queries, keys)


P_ROWS = 256


def _project_kernel(n_v, where, xa_ref, xb_ref, *refs):
    pieces, (o_ref,) = refs[:-1], refs[-1:]
    i = pl.program_id(0)

    def go(x_ref):
        at = 0
        for half, group in enumerate((pieces[:n_v], pieces[n_v:])):
            total = jnp.zeros((P_ROWS, WIDE), F32)
            for piece in group:
                for r in range(piece.shape[0] // 256):
                    c = pl.multiple_of(where[at] * 256, 256)
                    total += jnp.dot(
                        x_ref[:, pl.ds(c, 256)],
                        piece[r * 256 : (r + 1) * 256],
                        preferred_element_type=F32,
                    )
                    at += 1
            o_ref[half * WIDE : (half + 1) * WIDE] = total.T.astype(BF)

    steps = LEN // P_ROWS

    @pl.when(i < steps)
    def _():
        go(xa_ref)

    @pl.when(i >= steps)
    def _():
        go(xb_ref)


def project(where, xa, xb, v_pieces, t_pieces):
    steps = LEN // P_ROWS
    pieces = [*v_pieces, *t_pieces]
    depth = xa.shape[1]
    whole = [pl.BlockSpec(p.shape, lambda i, w: (0, 0)) for p in pieces]

    def kernel(*refs):
        _project_kernel(len(v_pieces), *refs)

    return pl.pallas_call(
        kernel,
        grid_spec=pltpu.PrefetchScalarGridSpec(
            num_scalar_prefetch=1,
            grid=(2 * steps,),
            in_specs=[
                pl.BlockSpec((P_ROWS, depth), lambda i, w: (jnp.minimum(i, steps - 1), 0)),
                pl.BlockSpec((P_ROWS, depth), lambda i, w: (jnp.maximum(i - steps, 0), 0)),
                *whole,
            ],
            out_specs=pl.BlockSpec((2 * WIDE, P_ROWS), lambda i, w: (0, i)),
        ),
        out_shape=jax.ShapeDtypeStruct((2 * WIDE, 2 * LEN), BF),
        compiler_params=_params(1),
        cost_estimate=pl.CostEstimate(
            flops=2 * LEN * depth * 2 * WIDE * 2,
            bytes_accessed=(2 * LEN * depth + depth * 2 * WIDE) * 2,
            transcendentals=0,
        ),
    )(where, xa, xb, *pieces)


H_STEP = 2


def _pull_kernel(p_ref, v_ref, t_ref, o_ref, acc):
    h = pl.program_id(1)

    @pl.when(h == 0)
    def _():
        acc[...] = jnp.zeros_like(acc)

    both = jnp.concatenate([v_ref[...], t_ref[...]], axis=0)

    def back(o):
        out, tan = o[:HD], o[HD:]
        square = jnp.sum(out * out, axis=0, keepdims=True) * (1.0 / HD)
        cross = jnp.sum(out * tan, axis=0, keepdims=True) * (1.0 / HD)
        inv2 = 1.0 / (square + EPSILON)
        pull = inv2 * cross * (1.0 + EPSILON * inv2)
        return (inv2 * (tan - out * pull)).astype(BF)

    for j in range(H_STEP):
        p0, p1 = p_ref[j, :HALF], p_ref[j, HALF:]
        w0 = back(jnp.dot(both[:, :HALF], p0, preferred_element_type=F32))
        w1 = back(jnp.dot(both, p1, preferred_element_type=F32))
        acc[:HALF] += lax.dot_general(p0, w0, NT, preferred_element_type=F32)
        acc[...] += lax.dot_general(p1, w1, NT, preferred_element_type=F32)

    @pl.when(h == PER // H_STEP - 1)
    def _():
        o_ref[...] = acc[...].T.astype(BF)


def pull_back(probs, projected, seq):
    steps = PER // H_STEP
    return pl.pallas_call(
        _pull_kernel,
        grid=(2, steps),
        in_specs=[
            pl.BlockSpec((H_STEP, 3 * HALF, HALF), lambda g, h: (g * steps + h, 0, 0)),
            pl.BlockSpec((HD, LEN), lambda g, h: (g, seq)),
            pl.BlockSpec((HD, LEN), lambda g, h: (2 + g, seq)),
        ],
        out_specs=pl.BlockSpec((HD, LEN), lambda g, h: (g, 0)),
        out_shape=jax.ShapeDtypeStruct((WIDE, LEN), BF),
        scratch_shapes=[pltpu.VMEM((LEN, HD), F32)],
        compiler_params=_params(2),
    )(probs, projected, projected)


G_COLS = 512
OWN = 128


def _ggn_kernel(pa_ref, pb_ref, xa_ref, xb_ref, o_ref):
    total = jnp.dot(pa_ref[...], xa_ref[...], preferred_element_type=F32)
    total += jnp.dot(pb_ref[...], xb_ref[...], preferred_element_type=F32)
    for j in range(G_COLS // OWN):
        o_ref[j] = total[:, j * OWN : (j + 1) * OWN].astype(BF)


def curvature(pa, pb, xa, xb):
    depth = xa.shape[1]
    return pl.pallas_call(
        _ggn_kernel,
        grid=(depth // G_COLS,),
        in_specs=[
            pl.BlockSpec((WIDE, LEN), lambda i: (0, 0)),
            pl.BlockSpec((WIDE, LEN), lambda i: (0, 0)),
            pl.BlockSpec((LEN, G_COLS), lambda i: (0, i)),
            pl.BlockSpec((LEN, G_COLS), lambda i: (0, i)),
        ],
        out_specs=pl.BlockSpec((G_COLS // OWN, WIDE, OWN), lambda i: (i, 0, 0)),
        out_shape=jax.ShapeDtypeStruct((depth // OWN, WIDE, OWN), BF),
        compiler_params=_params(1),
    )(pa, pb, xa, xb)


def hop(x, axis, by):
    return lax.ppermute(x, axis, [(i, (i + by) % 4) for i in range(4)])


def moved(places, axis, by):
    at = "xz".index(axis)
    return [tuple((v + by) % 4 if i == at else v for i, v in enumerate(p)) for p in places]


def ring(x, places, axis):
    half = x.shape[0] // 2
    cut = len(places) // 2
    before, after = hop(x, axis, 1), hop(x, axis, 3)
    far_a = hop(before[:half], axis, 1)
    far_b = hop(after[half:], axis, 3)
    arrays = [x, before, after, far_a, far_b]
    order = [
        places,
        moved(places, axis, -1),
        moved(places, axis, 1),
        moved(places[:cut], axis, 2),
        moved(places[cut:], axis, 2),
    ]
    return arrays, order


def gather_rows(value, tangent):
    rows = value.shape[0]
    joined = jnp.concatenate([value, tangent], axis=0)
    swapped = lax.ppermute(joined, ("yl", "yh"), Y_SWAP)
    value = jnp.concatenate([value, swapped[:rows]], axis=0)
    tangent = jnp.concatenate([tangent, swapped[rows:]], axis=0)
    places = [(0, 0, 0), (0, 0, 1)]
    result = []
    first = [ring(value, places, "x"), ring(tangent, places, "z")]
    for (arrays, order), axis in zip(first, "zx"):
        whole = jnp.concatenate(arrays, axis=0)
        arrays, order = ring(whole, sum(order, []), axis)
        result.append((arrays, sum(order, [])))
    x, z, yh = (lax.axis_index(a) for a in ("x", "z", "yh"))
    where = [
        ((x + p[0]) % 4) * 8 + ((z + p[1]) % 4) * 2 + (yh + p[2]) % 2
        for _, order in result
        for p in order
    ]
    return result[0][0], result[1][0], jnp.stack(where).astype(jnp.int32)


CHIPS = ("x", "z", "yh", "yl")


def body(normed, queries, keys, value_weight, iterate, residual, direction, damping):
    core, yl = lax.axis_index("c"), lax.axis_index("yl")
    other = 1 - core
    swap = [(0, 1), (1, 0)]
    heads = 2 * PER * HD

    def cols(a, which, width):
        return lax.dynamic_slice_in_dim(a, which * width, width, 1)

    value = cols(value_weight, core, WIDE)
    tangent = cols(direction, core, WIDE).astype(BF)
    v_pieces, t_pieces, where = gather_rows(value, tangent)
    queries_b = lax.ppermute(cols(queries, other, heads), "c", swap)
    keys_b = lax.ppermute(cols(keys, other, WIDE), "c", swap)
    normed_b = lax.ppermute(normed, "c", swap)
    probs_a = probs_of(core[None].astype(jnp.int32), queries, keys)
    probs_b = probs_of(jnp.zeros((1,), jnp.int32), queries_b, keys_b)
    projected = project(where, normed, normed_b, v_pieces, t_pieces)
    pulled_a = pull_back(probs_a, projected, 0)
    pulled_b = pull_back(probs_b, projected, 1)
    parts = curvature(pulled_a, pulled_b, normed, normed_b)
    parts = lax.all_to_all(parts, CHIPS, 0, 0, tiled=True)
    tokens_all = lax.axis_size(("c",) + CHIPS) * normed.shape[0]
    summed = jnp.sum(parts.astype(F32), axis=0).T

    def piece(a):
        return lax.dynamic_slice(a, (yl * OWN, core * WIDE), (OWN, WIDE))

    d, r = piece(direction), piece(residual)
    h = summed / tokens_all + damping[0] * d
    sums = jnp.stack([jnp.sum(r * r), jnp.sum(d * h), jnp.sum(r * h), jnp.sum(h * h)])
    everyone = ("c",) + CHIPS
    n = lax.axis_size(everyone)
    row = jnp.zeros((128,), F32).at[:4].set(sums)
    rows = jnp.broadcast_to(row[None], (n, 128))
    rows = lax.all_to_all(rows, everyone, 0, 0, tiled=True)
    total = jnp.sum(rows, axis=0)
    h_c = lax.ppermute(h, "c", swap)
    h_y = lax.ppermute(h, "yl", swap)
    h_yc = lax.ppermute(h, ("yl", "c"), [(i, 3 - i) for i in range(4)])

    def in_order(flag, a, b, axis):
        return jnp.where(
            flag == 0, jnp.concatenate([a, b], axis), jnp.concatenate([b, a], axis)
        )

    hdir = in_order(yl, in_order(core, h, h_c, 1), in_order(core, h_y, h_yc, 1), 0)
    rr, ph, rh, hh = total[0], total[1], total[2], total[3]
    step = rr / ph
    nn = rr - 2.0 * step * rh + step * step * hh
    new_iterate = iterate + step * direction
    new_residual = residual - step * hdir
    new_direction = new_residual + nn / rr * direction
    return (new_iterate, new_residual, new_direction)


def solution(mesh):
    fine = Mesh(
        mesh.devices.reshape(2, 2, 4, 4, 2), ("yl", "c", "x", "z", "yh")
    )
    tokens = P(("yl", "c", "x", "z", "yh"), None)
    rows = P(("x", "z", "yh"), None)
    return jax.shard_map(
        body,
        mesh=fine,
        in_specs=(tokens, tokens, tokens, rows, rows, rows, rows, P()),
        out_specs=(rows, rows, rows),
        check_vma=False,
    )
```

```python
import functools
import math

import jax
import jax.numpy as jnp
from jax import lax
from jax.experimental import pallas as pl
from jax.experimental.pallas import tpu as pltpu
from jax.sharding import Mesh, PartitionSpec as P

HD = 128
EPSILON = 1e-05
BF = jnp.bfloat16
F32 = jnp.float32
LEN = 512
HALF = 256
WIDE = 256
PER = 8
VMEM = 56 * 1024 * 1024
NT = (((1,), (1,)), ((), ()))
Y_SWAP = [(0, 3), (3, 0), (2, 1), (1, 2)]


def _params(n):
    return pltpu.CompilerParams(
        dimension_semantics=("arbitrary",) * n, vmem_limit_bytes=VMEM
    )


Q_STEP = 4


def _probs_kernel(off, qa_ref, ka_ref, qb_ref, kb_ref, p0_ref, p1_ref):
    del off
    factor = math.log2(math.e) / math.sqrt(HD)
    rows = lax.broadcasted_iota(jnp.int32, (HALF, HALF), 0)
    cols = lax.broadcasted_iota(jnp.int32, (HALF, HALF), 1)
    seen = rows <= cols

    def go(q_ref, k_ref):
        for j in range(Q_STEP):
            q = q_ref[:, j * HD : (j + 1) * HD]
            out = slice(j * HALF, (j + 1) * HALF)
            diag = lax.dot_general(
                k_ref[:HALF], q[:HALF], NT, preferred_element_type=F32
            )
            diag = jnp.where(seen, diag, -jnp.inf)
            top = jnp.max(diag, axis=0, keepdims=True)
            e = jnp.exp2((diag - top) * factor)
            inv = 1.0 / jnp.sum(e, axis=0, keepdims=True)
            p0_ref[:, out] = (e * inv).astype(BF)
            low = lax.dot_general(
                k_ref[:HALF], q[HALF:], NT, preferred_element_type=F32
            )
            diag = lax.dot_general(
                k_ref[HALF:], q[HALF:], NT, preferred_element_type=F32
            )
            diag = jnp.where(seen, diag, -jnp.inf)
            top = jnp.maximum(
                jnp.max(low, axis=0, keepdims=True),
                jnp.max(diag, axis=0, keepdims=True),
            )
            e = jnp.exp2((low - top) * factor)
            f = jnp.exp2((diag - top) * factor)
            inv = 1.0 / (
                jnp.sum(e, axis=0, keepdims=True) + jnp.sum(f, axis=0, keepdims=True)
            )
            p1_ref[:HALF, out] = (e * inv).astype(BF)
            p1_ref[HALF:, out] = (f * inv).astype(BF)

    @pl.when(pl.program_id(0) == 0)
    def _():
        go(qa_ref, ka_ref)

    @pl.when(pl.program_id(0) == 1)
    def _():
        go(qb_ref, kb_ref)


def probs_of(core, queries, keys, other):
    heads = 2 * PER
    steps = heads // Q_STEP
    per = steps // 2
    wide = Q_STEP * HALF

    def first(s, i):
        return jnp.where(s == 0, i, steps - 1)

    return pl.pallas_call(
        _probs_kernel,
        grid_spec=pltpu.PrefetchScalarGridSpec(
            num_scalar_prefetch=1,
            grid=(2, steps),
            in_specs=[
                pl.BlockSpec(
                    (LEN, Q_STEP * HD), lambda s, i, o: (0, o[0] * steps + first(s, i))
                ),
                pl.BlockSpec((LEN, HD), lambda s, i, o: (0, o[0] * 2 + first(s, i) // per)),
                pl.BlockSpec((LEN, Q_STEP * HD), lambda s, i, o: (0, s * i)),
                pl.BlockSpec((LEN, HD), lambda s, i, o: (0, heads + s * (i // per))),
            ],
            out_specs=[
                pl.BlockSpec((HALF, wide), lambda s, i, o: (0, s * steps + i)),
                pl.BlockSpec((LEN, wide), lambda s, i, o: (0, s * steps + i)),
            ],
        ),
        out_shape=[
            jax.ShapeDtypeStruct((HALF, 2 * heads * HALF), BF),
            jax.ShapeDtypeStruct((LEN, 2 * heads * HALF), BF),
        ],
        compiler_params=_params(2),
        cost_estimate=pl.CostEstimate(
            flops=2 * heads * 3 * HALF * HALF * HD * 2,
            bytes_accessed=2 * heads * (3 * HALF * HALF + LEN * HD) * 2,
            transcendentals=2 * heads * 3 * HALF * HALF,
        ),
    )(core, queries, keys, other, other)


SHARD = 256
P_STEP = 2


def _project_kernel(counts, first, last, where, *refs):
    del where
    xs, refs = refs[: 4 * P_STEP], refs[4 * P_STEP :]
    n = len(counts)
    streams, refs = (refs[:n], refs[n : 2 * n]), refs[2 * n :]
    k = pl.program_id(0)
    acc = refs[-1]

    @pl.when(k == 0)
    def _():
        acc[...] = jnp.zeros_like(acc) if first else refs[0][...]

    at = 0
    for i, count in enumerate(counts):

        @pl.when((k >= at) & (k < at + count))
        def _():
            deep = jnp.concatenate([streams[0][i][...], streams[1][i][...]], axis=0)
            for s in range(2):
                x = jnp.concatenate(
                    [r[...] for r in xs[s * 2 * P_STEP : (s + 1) * 2 * P_STEP]], axis=1
                )
                acc[s * LEN : (s + 1) * LEN] += jnp.dot(
                    x, deep, preferred_element_type=F32
                )

        at += count

    if last:

        @pl.when(k == at - 1)
        def _():
            for s in range(2):
                refs[-2][:, s * LEN : (s + 1) * LEN] = (
                    acc[s * LEN : (s + 1) * LEN].T.astype(BF)
                )


def project(where, xa, xb, a_pieces, b_pieces, before=None, last=False):
    deep = P_STEP * SHARD
    counts = [p.shape[0] // deep for p in a_pieces]
    n = sum(counts)
    first = before is None
    x_specs = [
        pl.BlockSpec(
            (LEN, SHARD), lambda k, w, c=c, j=j: (0, w[(c * n + k) * P_STEP + j])
        )
        for c in range(2)
        for j in range(P_STEP)
    ] * 2
    w_specs = [
        pl.BlockSpec(
            (deep, 2 * WIDE),
            lambda k, w, a=sum(counts[:i]), c=count: (jnp.clip(k - a, 0, c - 1), 0),
        )
        for i, count in enumerate(counts)
    ] * 2
    whole = pl.BlockSpec((2 * LEN, 2 * WIDE), lambda k, w: (0, 0))

    def kernel(*refs):
        _project_kernel(counts, first, last, *refs)

    return pl.pallas_call(
        kernel,
        grid_spec=pltpu.PrefetchScalarGridSpec(
            num_scalar_prefetch=1,
            grid=(n,),
            in_specs=[*x_specs, *w_specs, *([] if first else [whole])],
            out_specs=pl.BlockSpec((2 * WIDE, 2 * LEN), lambda k, w: (0, 0)) if last else whole,
            scratch_shapes=[pltpu.VMEM((2 * LEN, 2 * WIDE), F32)] if last else [],
        ),
        out_shape=jax.ShapeDtypeStruct((2 * WIDE, 2 * LEN), BF)
        if last
        else jax.ShapeDtypeStruct((2 * LEN, 2 * WIDE), F32),
        compiler_params=_params(1),
        cost_estimate=pl.CostEstimate(
            flops=2 * LEN * deep * 2 * n * 2 * WIDE * 2,
            bytes_accessed=n * deep * (4 * LEN + 4 * WIDE) * 2,
            transcendentals=0,
        ),
    )(
        where,
        *[xa] * (2 * P_STEP),
        *[xb] * (2 * P_STEP),
        *a_pieces,
        *b_pieces,
        *([] if first else [before]),
    )


H_STEP = 4


def _pull_kernel(p0_ref, p1_ref, v_ref, t_ref, o_ref, acc):
    h = pl.program_id(2)

    @pl.when(h == 0)
    def _():
        acc[...] = jnp.zeros_like(acc)

    both = jnp.concatenate([v_ref[...], t_ref[...]], axis=0)

    def back(o):
        out, tan = o[:HD], o[HD:]
        square = jnp.sum(out * out, axis=0, keepdims=True) * (1.0 / HD)
        cross = jnp.sum(out * tan, axis=0, keepdims=True) * (1.0 / HD)
        inv2 = 1.0 / (square + EPSILON)
        pull = inv2 * cross * (1.0 + EPSILON * inv2)
        return (inv2 * (tan - out * pull)).astype(BF)

    w0 = back(jnp.dot(both[:, :HALF], p0_ref[...], preferred_element_type=F32))
    w1 = back(jnp.dot(both, p1_ref[...], preferred_element_type=F32))
    acc[:HALF] += lax.dot_general(p0_ref[...], w0, NT, preferred_element_type=F32)
    acc[...] += lax.dot_general(p1_ref[...], w1, NT, preferred_element_type=F32)

    @pl.when(h == PER // H_STEP - 1)
    def _():
        o_ref[...] = acc[...].T.astype(BF)


def pull_back(p0, p1, projected):
    steps = PER // H_STEP
    wide = H_STEP * HALF
    return pl.pallas_call(
        _pull_kernel,
        grid=(2, 2, steps),
        in_specs=[
            pl.BlockSpec((HALF, wide), lambda s, g, h: (0, (s * 2 + g) * steps + h)),
            pl.BlockSpec((LEN, wide), lambda s, g, h: (0, (s * 2 + g) * steps + h)),
            pl.BlockSpec((HD, LEN), lambda s, g, h: (g, s)),
            pl.BlockSpec((HD, LEN), lambda s, g, h: (2 + g, s)),
        ],
        out_specs=pl.BlockSpec((HD, LEN), lambda s, g, h: (g, s)),
        out_shape=jax.ShapeDtypeStruct((WIDE, 2 * LEN), BF),
        scratch_shapes=[pltpu.VMEM((LEN, HD), F32)],
        compiler_params=_params(3),
    )(p0, p1, projected, projected)


G_COLS = 2048
OWN = 128


def _ggn_kernel(pa_ref, pb_ref, xa_ref, xb_ref, o_ref):
    total = jnp.dot(pa_ref[...], xa_ref[...], preferred_element_type=F32)
    total += jnp.dot(pb_ref[...], xb_ref[...], preferred_element_type=F32)
    for j in range(G_COLS // OWN):
        o_ref[j] = total[:, j * OWN : (j + 1) * OWN].astype(BF)


def curvature(pulled, xa, xb):
    depth = xa.shape[1]
    return pl.pallas_call(
        _ggn_kernel,
        grid=(depth // G_COLS,),
        in_specs=[
            pl.BlockSpec((WIDE, LEN), lambda i: (0, 0)),
            pl.BlockSpec((WIDE, LEN), lambda i: (0, 1)),
            pl.BlockSpec((LEN, G_COLS), lambda i: (0, i)),
            pl.BlockSpec((LEN, G_COLS), lambda i: (0, i)),
        ],
        out_specs=pl.BlockSpec((G_COLS // OWN, WIDE, OWN), lambda i: (i, 0, 0)),
        out_shape=jax.ShapeDtypeStruct((depth // OWN, WIDE, OWN), BF),
        compiler_params=_params(1),
    )(pulled, pulled, xa, xb)


ANY = pl.BlockSpec(memory_space=pl.ANY)
WHOLE = pl.BlockSpec(memory_space=pltpu.VMEM)


def narrow(core, value, direction):
    def kernel(core_ref, value_ref, direction_ref, o_ref):
        del core_ref
        o_ref[:, :WIDE] = value_ref[...]
        o_ref[:, WIDE:] = direction_ref[...].astype(BF)

    rows = value.shape[0]
    part = pl.BlockSpec((rows, WIDE), lambda i, c: (0, c[0]))
    return pl.pallas_call(
        kernel,
        grid_spec=pltpu.PrefetchScalarGridSpec(
            num_scalar_prefetch=1,
            grid=(1,),
            in_specs=[part, part],
            out_specs=pl.BlockSpec((rows, 2 * WIDE), lambda i, c: (0, 0)),
        ),
        out_shape=jax.ShapeDtypeStruct((rows, 2 * WIDE), BF),
        compiler_params=_params(1),
    )(core, value, direction)


def chosen(yh, own, swapped, after):
    def kernel(yh_ref, own_ref, swapped_ref, _, low_ref, high_ref, zero_ref):
        zero_ref[0] = 0

        @pl.when(yh_ref[0] == 0)
        def _():
            low_ref[...] = own_ref[...]
            high_ref[...] = swapped_ref[...]

        @pl.when(yh_ref[0] != 0)
        def _():
            low_ref[...] = swapped_ref[...]
            high_ref[...] = own_ref[...]

    return pl.pallas_call(
        kernel,
        in_specs=[pl.BlockSpec(memory_space=pltpu.SMEM), WHOLE, WHOLE, ANY],
        out_specs=[WHOLE, WHOLE, pl.BlockSpec(memory_space=pltpu.SMEM)],
        out_shape=[jax.ShapeDtypeStruct(own.shape, BF)] * 2
        + [jax.ShapeDtypeStruct((1,), jnp.int32)],
        compiler_params=pltpu.CompilerParams(vmem_limit_bytes=VMEM),
    )(yh, own, swapped, after)


def halves(arrays, after):
    n = len(arrays)
    half = arrays[0].shape[0] // 2
    steps = max(half // 256, 1)
    rows = half // steps

    def kernel(*refs):
        for a, o in zip(refs[:n], refs[-n:]):
            o[...] = a[...]

    shape = (rows, arrays[0].shape[1])
    return pl.pallas_call(
        kernel,
        grid=(steps,),
        in_specs=[
            pl.BlockSpec(shape, lambda i, c=c % 2: (i + c * steps, 0)) for c in range(n)
        ]
        + [ANY] * len(after),
        out_specs=[pl.BlockSpec(shape, lambda i: (i, 0))] * n,
        out_shape=[jax.ShapeDtypeStruct((half, shape[1]), BF)] * n,
        compiler_params=_params(1),
    )(*arrays, *after)


def joined(lists):
    flat = sum(lists, [])

    def kernel(*refs):
        at = 0
        for arrays, o in zip(lists, refs[len(flat) :]):
            row = 0
            for _ in arrays:
                n = refs[at].shape[0]
                o[row : row + n] = refs[at][...]
                row, at = row + n, at + 1

    return pl.pallas_call(
        kernel,
        in_specs=[WHOLE] * len(flat),
        out_specs=[WHOLE] * len(lists),
        out_shape=[
            jax.ShapeDtypeStruct((sum(a.shape[0] for a in l), l[0].shape[1]), BF)
            for l in lists
        ],
        compiler_params=pltpu.CompilerParams(vmem_limit_bytes=VMEM),
    )(*flat)


def hop(x, axis, by):
    return lax.ppermute(x, axis, [(i, (i + by) % 4) for i in range(4)])


def rings(arrays, axes, after):
    near = [hop(x, a, by) for x, a in zip(arrays, axes) for by in (1, 3)]
    cut = halves(near, after)
    far = [hop(h, axes[i // 2], (1, 3)[i % 2]) for i, h in enumerate(cut)]
    return [(x, *near[2 * i : 2 * i + 2], *far[2 * i : 2 * i + 2]) for i, x in enumerate(arrays)]


S_STEP = 16


def _share_kernel(at_ref, damping_ref, parts_ref, d_ref, r_ref, h_ref, row_ref, acc, *, tokens):
    del at_ref
    i = pl.program_id(0)

    @pl.when(i == 0)
    def _():
        acc[...] = jnp.zeros_like(acc)

    acc[...] += jnp.sum(parts_ref[...].astype(F32), axis=0)

    @pl.when(i == pl.num_programs(0) - 1)
    def _():
        d, r = d_ref[...], r_ref[...]
        h = acc[...].T * (1.0 / tokens) + damping_ref[0] * d
        h_ref[...] = h
        lane = lax.broadcasted_iota(jnp.int32, row_ref.shape, 1)
        row = jnp.zeros(row_ref.shape, F32)
        for j, term in enumerate((r * r, d * h, r * h, h * h)):
            row = jnp.where(lane == j, jnp.sum(term), row)
        row_ref[...] = row


def share(at, damping, parts, direction, residual, devices, tokens):
    n = parts.shape[0] // S_STEP
    own = pl.BlockSpec((OWN, WIDE), lambda i, w: (w[0], w[1]))
    return pl.pallas_call(
        functools.partial(_share_kernel, tokens=tokens),
        grid_spec=pltpu.PrefetchScalarGridSpec(
            num_scalar_prefetch=1,
            grid=(n,),
            in_specs=[
                pl.BlockSpec(memory_space=pltpu.SMEM),
                pl.BlockSpec((S_STEP, WIDE, OWN), lambda i, w: (i, 0, 0)),
                own,
                own,
            ],
            out_specs=[
                pl.BlockSpec((OWN, WIDE), lambda i, w: (0, 0)),
                pl.BlockSpec((devices, 128), lambda i, w: (0, 0)),
            ],
            scratch_shapes=[pltpu.VMEM((WIDE, OWN), F32)],
        ),
        out_shape=[
            jax.ShapeDtypeStruct((OWN, WIDE), F32),
            jax.ShapeDtypeStruct((devices, 128), F32),
        ],
        compiler_params=_params(1),
    )(at, damping, parts, direction, residual)


CHIPS = ("x", "z", "yh", "yl")


def body(normed, queries, keys, value_weight, iterate, residual, direction, damping):
    core, yl = lax.axis_index("c"), lax.axis_index("yl")
    x, z, yh = (lax.axis_index(a) for a in ("x", "z", "yh"))
    other = 1 - core
    swap = [(0, 1), (1, 0)]
    heads = 2 * PER * HD

    def cols(a, which, width):
        return lax.dynamic_slice_in_dim(a, which * width, width, 1)

    own = narrow(core[None], value_weight, direction)
    normed_b = lax.ppermute(normed, "c", swap)
    swapped = lax.ppermute(own, ("yl", "yh"), Y_SWAP)
    *near, _ = chosen(yh[None], own, swapped, own)
    *far, zero = chosen(yh[None], own, swapped, normed_b)
    later = other + zero[0]
    partner = jnp.concatenate([cols(queries, later, heads), cols(keys, later, WIDE)], 1)
    partner = lax.ppermute(partner, "c", swap)
    inner = [
        [a, hop(a, axis, 1), hop(a, axis, 3), hop(b, axis, 2)]
        for a, b, axis in zip(near, far, "xz")
    ]
    lines = joined(inner)
    p0, p1 = probs_of(core[None], queries, keys, partner)
    turn = (0, -1, 1, 2)

    def places(steps):
        a_at = [((x + i) % 4) * 8 + (z + s) % 4 * 2 for s in steps for i in turn]
        b_at = [((x + s) % 4) * 8 + (z + i) % 4 * 2 + 1 for s in steps for i in turn]
        return jnp.stack(a_at + b_at).astype(jnp.int32)

    some = project(places((0,)), normed, normed_b, lines[:1], lines[1:])
    (_, *a, a_far, a_far2), (_, *b, b_far, b_far2) = rings(lines, "zx", [p0, some])
    most = project(places((-1, 1)), normed, normed_b, a, b, some)
    projected = project(
        places((2,)), normed, normed_b, [a_far, a_far2], [b_far, b_far2], most, True
    )
    pulled = pull_back(p0, p1, projected)
    parts = curvature(pulled, normed, normed_b)
    parts = lax.all_to_all(parts, CHIPS, 0, 0, tiled=True)
    everyone = ("c",) + CHIPS
    devices = lax.axis_size(everyone)
    h, rows = share(
        jnp.stack([yl, core]), damping, parts, direction, residual, devices, devices * normed.shape[0]
    )
    rows = lax.all_to_all(rows, everyone, 0, 0, tiled=True)
    total = jnp.sum(rows, axis=0)
    h_c = lax.ppermute(h, "c", swap)
    h_y = lax.ppermute(h, "yl", swap)
    h_yc = lax.ppermute(h, ("yl", "c"), [(i, 3 - i) for i in range(4)])

    def in_order(flag, a, b, axis):
        return jnp.where(
            flag == 0, jnp.concatenate([a, b], axis), jnp.concatenate([b, a], axis)
        )

    hdir = in_order(yl, in_order(core, h, h_c, 1), in_order(core, h_y, h_yc, 1), 0)
    rr, ph, rh, hh = total[0], total[1], total[2], total[3]
    step = rr / ph
    nn = rr - 2.0 * step * rh + step * step * hh
    new_iterate = iterate + step * direction
    new_residual = residual - step * hdir
    new_direction = new_residual + nn / rr * direction
    return (new_iterate, new_residual, new_direction)


def solution(mesh):
    fine = Mesh(
        mesh.devices.reshape(2, 2, 4, 4, 2), ("yl", "c", "x", "z", "yh")
    )
    tokens = P(("yl", "c", "x", "z", "yh"), None)
    rows = P(("x", "z", "yh"), None)
    return jax.shard_map(
        body,
        mesh=fine,
        in_specs=(tokens, tokens, tokens, rows, rows, rows, rows, P()),
        out_specs=(rows, rows, rows),
        check_vma=False,
    )
```

```python
import functools
import math

import jax
import jax.numpy as jnp
from jax import lax
from jax.experimental import pallas as pl
from jax.experimental.pallas import tpu as pltpu
from jax.sharding import Mesh, PartitionSpec as P

HD = 128
EPSILON = 1e-05
BF = jnp.bfloat16
F32 = jnp.float32
LEN = 512
HALF = 256
WIDE = 256
PER = 8
VMEM = 16 * 1024 * 1024
NT = (((1,), (1,)), ((), ()))
TOKEN = pl.BlockSpec(memory_space=pltpu.SMEM)
Y_SWAP = [(0, 3), (3, 0), (2, 1), (1, 2)]


def _params(n):
    return pltpu.CompilerParams(
        dimension_semantics=("arbitrary",) * n, vmem_limit_bytes=VMEM
    )


Q_STEP = 4


def _probs_kernel(off, q_ref, k_ref, p0_ref, p1_ref, token):
    del off
    token[0] = 0
    factor = math.log2(math.e) / math.sqrt(HD)
    rows = lax.broadcasted_iota(jnp.int32, (HALF, HALF), 0)
    cols = lax.broadcasted_iota(jnp.int32, (HALF, HALF), 1)
    seen = rows <= cols

    for j in range(Q_STEP):
        q = q_ref[:, j * HD : (j + 1) * HD]
        out = slice(j * HALF, (j + 1) * HALF)
        diag = lax.dot_general(
            k_ref[:HALF], q[:HALF], NT, preferred_element_type=F32
        )
        diag = jnp.where(seen, diag, -jnp.inf)
        top = jnp.max(diag, axis=0, keepdims=True)
        e = jnp.exp2((diag - top) * factor)
        inv = 1.0 / jnp.sum(e, axis=0, keepdims=True)
        p0_ref[:, out] = (e * inv).astype(BF)
        low = lax.dot_general(
            k_ref[:HALF], q[HALF:], NT, preferred_element_type=F32
        )
        diag = lax.dot_general(
            k_ref[HALF:], q[HALF:], NT, preferred_element_type=F32
        )
        diag = jnp.where(seen, diag, -jnp.inf)
        top = jnp.maximum(
            jnp.max(low, axis=0, keepdims=True),
            jnp.max(diag, axis=0, keepdims=True),
        )
        e = jnp.exp2((low - top) * factor)
        f = jnp.exp2((diag - top) * factor)
        inv = 1.0 / (
            jnp.sum(e, axis=0, keepdims=True) + jnp.sum(f, axis=0, keepdims=True)
        )
        p1_ref[:HALF, out] = (e * inv).astype(BF)
        p1_ref[HALF:, out] = (f * inv).astype(BF)


def probs_of(at, queries, keys):
    heads = 2 * PER
    steps = heads // Q_STEP
    per = steps // 2
    wide = Q_STEP * HALF
    return pl.pallas_call(
        _probs_kernel,
        grid_spec=pltpu.PrefetchScalarGridSpec(
            num_scalar_prefetch=1,
            grid=(steps,),
            in_specs=[
                pl.BlockSpec((LEN, Q_STEP * HD), lambda i, o: (0, o[0] + i)),
                pl.BlockSpec((LEN, HD), lambda i, o: (0, o[1] + i // per)),
            ],
            out_specs=[
                pl.BlockSpec((HALF, wide), lambda i, o: (0, i)),
                pl.BlockSpec((LEN, wide), lambda i, o: (0, i)),
                TOKEN,
            ],
        ),
        out_shape=[
            pltpu.HBM((HALF, heads * HALF), BF),
            pltpu.HBM((LEN, heads * HALF), BF),
            jax.ShapeDtypeStruct((1,), jnp.int32),
        ],
        compiler_params=_params(1),
        cost_estimate=pl.CostEstimate(
            flops=heads * 3 * HALF * HALF * HD * 2,
            bytes_accessed=heads * (3 * HALF * HALF + LEN * HD) * 2,
            transcendentals=heads * 3 * HALF * HALF,
        ),
    )(at, queries, keys)


SHARD = 256
P_STEP = 2


def _project_kernel(counts, first, last, where, *refs):
    del where
    xs, refs = refs[: 4 * P_STEP], refs[4 * P_STEP :]
    n = len(counts)
    streams, refs = (refs[:n], refs[n : 2 * n]), refs[2 * n :]
    k = pl.program_id(0)
    if not last:
        refs[-1][0] = 0
        refs = refs[:-1]
    acc = refs[-1]

    @pl.when(k == 0)
    def _():
        acc[...] = jnp.zeros_like(acc) if first else refs[0][...]

    at = 0
    for i, count in enumerate(counts):

        @pl.when((k >= at) & (k < at + count))
        def _():
            deep = jnp.concatenate([streams[0][i][...], streams[1][i][...]], axis=0)
            for s in range(2):
                x = jnp.concatenate(
                    [r[...] for r in xs[s * 2 * P_STEP : (s + 1) * 2 * P_STEP]], axis=1
                )
                acc[s * LEN : (s + 1) * LEN] += jnp.dot(
                    x, deep, preferred_element_type=F32
                )

        at += count

    if last:

        @pl.when(k == at - 1)
        def _():
            for s in range(2):
                refs[-2][:, s * LEN : (s + 1) * LEN] = (
                    acc[s * LEN : (s + 1) * LEN].T.astype(BF)
                )


def project(where, xa, xb, a_pieces, b_pieces, before=None, last=False):
    deep = P_STEP * SHARD
    counts = [p.shape[0] // deep for p in a_pieces]
    n = sum(counts)
    first = before is None
    x_specs = [
        pl.BlockSpec(
            (LEN, SHARD), lambda k, w, c=c, j=j: (0, w[(c * n + k) * P_STEP + j])
        )
        for c in range(2)
        for j in range(P_STEP)
    ] * 2
    w_specs = [
        pl.BlockSpec(
            (deep, 2 * WIDE),
            lambda k, w, a=sum(counts[:i]), c=count: (jnp.clip(k - a, 0, c - 1), 0),
        )
        for i, count in enumerate(counts)
    ] * 2
    whole = pl.BlockSpec((2 * LEN, 2 * WIDE), lambda k, w: (0, 0))

    def kernel(*refs):
        _project_kernel(counts, first, last, *refs)

    return pl.pallas_call(
        kernel,
        grid_spec=pltpu.PrefetchScalarGridSpec(
            num_scalar_prefetch=1,
            grid=(n,),
            in_specs=[*x_specs, *w_specs, *([] if first else [whole])],
            out_specs=pl.BlockSpec((2 * WIDE, 2 * LEN), lambda k, w: (0, 0)) if last else [whole, TOKEN],
            scratch_shapes=[pltpu.VMEM((2 * LEN, 2 * WIDE), F32)] if last else [],
        ),
        out_shape=jax.ShapeDtypeStruct((2 * WIDE, 2 * LEN), BF)
        if last
        else [
            (pltpu.HBM if first else jax.ShapeDtypeStruct)((2 * LEN, 2 * WIDE), F32),
            jax.ShapeDtypeStruct((1,), jnp.int32),
        ],
        compiler_params=_params(1),
        cost_estimate=pl.CostEstimate(
            flops=2 * LEN * deep * 2 * n * 2 * WIDE * 2,
            bytes_accessed=n * deep * (4 * LEN + 4 * WIDE) * 2,
            transcendentals=0,
        ),
    )(
        where,
        *[xa] * (2 * P_STEP),
        *[xb] * (2 * P_STEP),
        *a_pieces,
        *b_pieces,
        *([] if first else [before]),
    )


H_STEP = 4


def _pull_kernel(a0_ref, a1_ref, b0_ref, b1_ref, v_ref, t_ref, o_ref, acc):
    s, h = pl.program_id(0), pl.program_id(2)

    @pl.when(h == 0)
    def _():
        acc[...] = jnp.zeros_like(acc)

    def back(o):
        out, tan = o[:HD], o[HD:]
        square = jnp.sum(out * out, axis=0, keepdims=True) * (1.0 / HD)
        cross = jnp.sum(out * tan, axis=0, keepdims=True) * (1.0 / HD)
        inv2 = 1.0 / (square + EPSILON)
        pull = inv2 * cross * (1.0 + EPSILON * inv2)
        return (inv2 * (tan - out * pull)).astype(BF)

    def go(p0_ref, p1_ref):
        both = jnp.concatenate([v_ref[...], t_ref[...]], axis=0)
        w0 = back(jnp.dot(both[:, :HALF], p0_ref[...], preferred_element_type=F32))
        w1 = back(jnp.dot(both, p1_ref[...], preferred_element_type=F32))
        acc[:HALF] += lax.dot_general(p0_ref[...], w0, NT, preferred_element_type=F32)
        acc[...] += lax.dot_general(p1_ref[...], w1, NT, preferred_element_type=F32)

    @pl.when(s == 0)
    def _():
        go(a0_ref, a1_ref)

    @pl.when(s == 1)
    def _():
        go(b0_ref, b1_ref)

    @pl.when(h == PER // H_STEP - 1)
    def _():
        o_ref[...] = acc[...].T.astype(BF)


def pull_back(a0, a1, b0, b1, projected):
    steps = PER // H_STEP
    wide = H_STEP * HALF

    def in_a(s, g, h):
        return 0, jnp.where(s == 0, g * steps + h, 2 * steps - 1)

    def in_b(s, g, h):
        return 0, s * (g * steps + h)

    return pl.pallas_call(
        _pull_kernel,
        grid=(2, 2, steps),
        in_specs=[
            pl.BlockSpec((HALF, wide), in_a),
            pl.BlockSpec((LEN, wide), in_a),
            pl.BlockSpec((HALF, wide), in_b),
            pl.BlockSpec((LEN, wide), in_b),
            pl.BlockSpec((HD, LEN), lambda s, g, h: (g, s)),
            pl.BlockSpec((HD, LEN), lambda s, g, h: (2 + g, s)),
        ],
        out_specs=pl.BlockSpec((HD, LEN), lambda s, g, h: (g, s)),
        out_shape=jax.ShapeDtypeStruct((WIDE, 2 * LEN), BF),
        scratch_shapes=[pltpu.VMEM((LEN, HD), F32)],
        compiler_params=_params(3),
    )(a0, a1, b0, b1, projected, projected)


G_COLS = 2048
OWN = 128


def _ggn_kernel(pa_ref, pb_ref, xa_ref, xb_ref, o_ref):
    total = jnp.dot(pa_ref[...], xa_ref[...], preferred_element_type=F32)
    total += jnp.dot(pb_ref[...], xb_ref[...], preferred_element_type=F32)
    for j in range(G_COLS // OWN):
        o_ref[j] = total[:, j * OWN : (j + 1) * OWN].astype(BF)


def curvature(pulled, xa, xb):
    depth = xa.shape[1]
    return pl.pallas_call(
        _ggn_kernel,
        grid=(depth // G_COLS,),
        in_specs=[
            pl.BlockSpec((WIDE, LEN), lambda i: (0, 0)),
            pl.BlockSpec((WIDE, LEN), lambda i: (0, 1)),
            pl.BlockSpec((LEN, G_COLS), lambda i: (0, i)),
            pl.BlockSpec((LEN, G_COLS), lambda i: (0, i)),
        ],
        out_specs=pl.BlockSpec((G_COLS // OWN, WIDE, OWN), lambda i: (i, 0, 0)),
        out_shape=pltpu.HBM((depth // OWN, WIDE, OWN), BF),
        compiler_params=_params(1),
    )(pulled, pulled, xa, xb)


ANY = pl.BlockSpec(memory_space=pl.ANY)
WHOLE = pl.BlockSpec(memory_space=pltpu.VMEM)


def narrow(core, value, direction):
    def kernel(core_ref, value_ref, direction_ref, o_ref):
        del core_ref
        o_ref[:, :WIDE] = value_ref[...]
        o_ref[:, WIDE:] = direction_ref[...].astype(BF)

    rows = value.shape[0]
    part = pl.BlockSpec((rows, WIDE), lambda i, c: (0, c[0]))
    return pl.pallas_call(
        kernel,
        grid_spec=pltpu.PrefetchScalarGridSpec(
            num_scalar_prefetch=1,
            grid=(1,),
            in_specs=[part, part],
            out_specs=pl.BlockSpec((rows, 2 * WIDE), lambda i, c: (0, 0)),
        ),
        out_shape=jax.ShapeDtypeStruct((rows, 2 * WIDE), BF),
        compiler_params=_params(1),
    )(core, value, direction)


def chosen(yh, own, swapped, after):
    def kernel(yh_ref, own_ref, swapped_ref, _, low_ref, high_ref):
        @pl.when(yh_ref[0] == 0)
        def _():
            low_ref[...] = own_ref[...]
            high_ref[...] = swapped_ref[...]

        @pl.when(yh_ref[0] != 0)
        def _():
            low_ref[...] = swapped_ref[...]
            high_ref[...] = own_ref[...]

    return pl.pallas_call(
        kernel,
        in_specs=[pl.BlockSpec(memory_space=pltpu.SMEM), WHOLE, WHOLE, ANY],
        out_specs=[WHOLE, WHOLE],
        out_shape=[jax.ShapeDtypeStruct(own.shape, BF)] * 2,
        compiler_params=pltpu.CompilerParams(vmem_limit_bytes=VMEM),
    )(yh, own, swapped, after)


def halves(arrays, after):
    n = len(arrays)
    half = arrays[0].shape[0] // 2
    steps = max(half // 256, 1)
    rows = half // steps

    def kernel(*refs):
        for a, o in zip(refs[:n], refs[-n:]):
            o[...] = a[...]

    shape = (rows, arrays[0].shape[1])
    return pl.pallas_call(
        kernel,
        grid=(steps,),
        in_specs=[
            pl.BlockSpec(shape, lambda i, c=c % 2: (i + c * steps, 0)) for c in range(n)
        ]
        + [TOKEN] * len(after),
        out_specs=[pl.BlockSpec(shape, lambda i: (i, 0))] * n,
        out_shape=[jax.ShapeDtypeStruct((half, shape[1]), BF)] * n,
        compiler_params=_params(1),
    )(*arrays, *after)


def joined(lists, after):
    flat = sum(lists, [])

    def kernel(*refs):
        at = 0
        for arrays, o in zip(lists, refs[-len(lists) :]):
            row = 0
            for _ in arrays:
                n = refs[at].shape[0]
                o[row : row + n] = refs[at][...]
                row, at = row + n, at + 1

    return pl.pallas_call(
        kernel,
        in_specs=[WHOLE] * len(flat) + [TOKEN] * len(after),
        out_specs=[WHOLE] * len(lists),
        out_shape=[
            jax.ShapeDtypeStruct((sum(a.shape[0] for a in l), l[0].shape[1]), BF)
            for l in lists
        ],
        compiler_params=pltpu.CompilerParams(vmem_limit_bytes=VMEM),
    )(*flat, *after)


def for_partner(other, queries, keys, after):
    wide = 2 * PER * HD

    def kernel(other_ref, q_ref, k_ref, _, o_ref):
        del other_ref
        o_ref[:, :wide] = q_ref[...]
        o_ref[:, wide:] = k_ref[...]

    return pl.pallas_call(
        kernel,
        grid_spec=pltpu.PrefetchScalarGridSpec(
            num_scalar_prefetch=1,
            grid=(1,),
            in_specs=[
                pl.BlockSpec((LEN, wide), lambda i, o: (0, o[0])),
                pl.BlockSpec((LEN, WIDE), lambda i, o: (0, o[0])),
                ANY,
            ],
            out_specs=pl.BlockSpec((LEN, wide + WIDE), lambda i, o: (0, 0)),
        ),
        out_shape=jax.ShapeDtypeStruct((LEN, wide + WIDE), BF),
        compiler_params=_params(1),
    )(other, queries, keys, after)


def hop(x, axis, by):
    return lax.ppermute(x, axis, [(i, (i + by) % 4) for i in range(4)])


def rings(arrays, axes, after):
    near = [hop(x, a, by) for x, a in zip(arrays, axes) for by in (1, 3)]
    cut = halves(near, after)
    far = [hop(h, axes[i // 2], (1, 3)[i % 2]) for i, h in enumerate(cut)]
    return [(x, *near[2 * i : 2 * i + 2], *far[2 * i : 2 * i + 2]) for i, x in enumerate(arrays)]


S_STEP = 16


def _share_kernel(at_ref, damping_ref, parts_ref, d_ref, r_ref, h_ref, row_ref, acc, *, tokens):
    del at_ref
    i = pl.program_id(0)

    @pl.when(i == 0)
    def _():
        acc[...] = jnp.zeros_like(acc)

    acc[...] += jnp.sum(parts_ref[...].astype(F32), axis=0)

    @pl.when(i == pl.num_programs(0) - 1)
    def _():
        d, r = d_ref[...], r_ref[...]
        h = acc[...].T * (1.0 / tokens) + damping_ref[0] * d
        h_ref[...] = h
        lane = lax.broadcasted_iota(jnp.int32, row_ref.shape, 1)
        row = jnp.zeros(row_ref.shape, F32)
        for j, term in enumerate((r * r, d * h, r * h, h * h)):
            row = jnp.where(lane == j, jnp.sum(term), row)
        row_ref[...] = row


def share(at, damping, parts, direction, residual, devices, tokens):
    n = parts.shape[0] // S_STEP
    own = pl.BlockSpec((OWN, WIDE), lambda i, w: (w[0], w[1]))
    return pl.pallas_call(
        functools.partial(_share_kernel, tokens=tokens),
        grid_spec=pltpu.PrefetchScalarGridSpec(
            num_scalar_prefetch=1,
            grid=(n,),
            in_specs=[
                pl.BlockSpec(memory_space=pltpu.SMEM),
                pl.BlockSpec((S_STEP, WIDE, OWN), lambda i, w: (i, 0, 0)),
                own,
                own,
            ],
            out_specs=[
                pl.BlockSpec((OWN, WIDE), lambda i, w: (0, 0)),
                pl.BlockSpec((devices, 128), lambda i, w: (0, 0)),
            ],
            scratch_shapes=[pltpu.VMEM((WIDE, OWN), F32)],
        ),
        out_shape=[
            jax.ShapeDtypeStruct((OWN, WIDE), F32),
            jax.ShapeDtypeStruct((devices, 128), F32),
        ],
        compiler_params=_params(1),
    )(at, damping, parts, direction, residual)


CHIPS = ("x", "z", "yh", "yl")


def body(normed, queries, keys, value_weight, iterate, residual, direction, damping):
    core, yl = lax.axis_index("c"), lax.axis_index("yl")
    x, z, yh = (lax.axis_index(a) for a in ("x", "z", "yh"))
    other = 1 - core
    swap = [(0, 1), (1, 0)]

    own = narrow(core[None], value_weight, direction)
    normed_b = lax.ppermute(normed, "c", swap)
    swapped = lax.ppermute(own, ("yl", "yh"), Y_SWAP)
    inner = [
        [a, *(hop(a, axis, by) for by in (1, 3, 2))]
        for a, axis in zip(chosen(yh[None], own, swapped, normed_b), "xz")
    ]
    *probs_a, done_a = probs_of(jnp.stack([core * 4, core * 2]), queries, keys)
    lines = joined(inner, [done_a])
    partner = lax.ppermute(for_partner(other[None], queries, keys, lines[0]), "c", swap)
    *probs_b, done_b = probs_of(jnp.array([0, 2 * PER], jnp.int32), partner, partner)
    turn = (0, -1, 1, 2)

    def places(steps):
        a_at = [((x + i) % 4) * 8 + (z + s) % 4 * 2 for s in steps for i in turn]
        b_at = [((x + s) % 4) * 8 + (z + i) % 4 * 2 + 1 for s in steps for i in turn]
        return jnp.stack(a_at + b_at).astype(jnp.int32)

    held = pltpu.with_memory_space_constraint(normed, pltpu.HBM)
    some, done_some = project(places((0,)), held, normed_b, lines[:1], lines[1:])
    (_, *a, a_far, a_far2), (_, *b, b_far, b_far2) = rings(lines, "zx", [done_b, done_some])
    most, _ = project(places((-1, 1)), held, normed_b, a, b, some)
    projected = project(
        places((2,)), held, normed_b, [a_far, a_far2], [b_far, b_far2], most, True
    )
    pulled = pull_back(*probs_a, *probs_b, projected)
    parts = curvature(pulled, normed, normed_b)
    parts = lax.all_to_all(parts, CHIPS, 0, 0, tiled=True)
    everyone = ("c",) + CHIPS
    devices = lax.axis_size(everyone)
    h, rows = share(
        jnp.stack([yl, core]), damping, parts, direction, residual, devices, devices * normed.shape[0]
    )
    rows = lax.all_to_all(rows, everyone, 0, 0, tiled=True)
    total = jnp.sum(rows, axis=0)
    h_c = lax.ppermute(h, "c", swap)
    h_y = lax.ppermute(h, "yl", swap)
    h_yc = lax.ppermute(h, ("yl", "c"), [(i, 3 - i) for i in range(4)])

    def in_order(flag, a, b, axis):
        return jnp.where(
            flag == 0, jnp.concatenate([a, b], axis), jnp.concatenate([b, a], axis)
        )

    hdir = in_order(yl, in_order(core, h, h_c, 1), in_order(core, h_y, h_yc, 1), 0)
    rr, ph, rh, hh = total[0], total[1], total[2], total[3]
    step = rr / ph
    nn = rr - 2.0 * step * rh + step * step * hh
    new_iterate = iterate + step * direction
    new_residual = residual - step * hdir
    new_direction = new_residual + nn / rr * direction
    return (new_iterate, new_residual, new_direction)


def solution(mesh):
    fine = Mesh(
        mesh.devices.reshape(2, 2, 4, 4, 2), ("yl", "c", "x", "z", "yh")
    )
    tokens = P(("yl", "c", "x", "z", "yh"), None)
    rows = P(("x", "z", "yh"), None)
    return jax.shard_map(
        body,
        mesh=fine,
        in_specs=(tokens, tokens, tokens, rows, rows, rows, rows, P()),
        out_specs=(rows, rows, rows),
        check_vma=False,
    )
```

```python
import functools
import math

import jax
import jax.numpy as jnp
from jax import lax
from jax.experimental import pallas as pl
from jax.experimental.pallas import tpu as pltpu
from jax.sharding import Mesh, PartitionSpec as P

HD = 128
EPSILON = 1e-05
BF = jnp.bfloat16
F32 = jnp.float32
LEN = 512
HALF = 256
WIDE = 256
PER = 8
VMEM = 16 * 1024 * 1024
NT = (((1,), (1,)), ((), ()))
TOKEN = pl.BlockSpec(memory_space=pltpu.SMEM)
Y_SWAP = [(0, 3), (3, 0), (2, 1), (1, 2)]


def _params(n):
    return pltpu.CompilerParams(
        dimension_semantics=("arbitrary",) * n, vmem_limit_bytes=VMEM
    )


Q_STEP = 4


def _probs_kernel(off, q_ref, k_ref, p0_ref, p1_ref, token):
    del off
    token[0] = 0
    factor = math.log2(math.e) / math.sqrt(HD)
    rows = lax.broadcasted_iota(jnp.int32, (HALF, HALF), 0)
    cols = lax.broadcasted_iota(jnp.int32, (HALF, HALF), 1)
    seen = rows <= cols

    for j in range(Q_STEP):
        q = q_ref[:, j * HD : (j + 1) * HD]
        out = slice(j * HALF, (j + 1) * HALF)
        diag = lax.dot_general(
            k_ref[:HALF], q[:HALF], NT, preferred_element_type=F32
        )
        diag = jnp.where(seen, diag, -jnp.inf)
        top = jnp.max(diag, axis=0, keepdims=True)
        e = jnp.exp2((diag - top) * factor)
        inv = 1.0 / jnp.sum(e, axis=0, keepdims=True)
        p0_ref[:, out] = (e * inv).astype(BF)
        low = lax.dot_general(
            k_ref[:HALF], q[HALF:], NT, preferred_element_type=F32
        )
        diag = lax.dot_general(
            k_ref[HALF:], q[HALF:], NT, preferred_element_type=F32
        )
        diag = jnp.where(seen, diag, -jnp.inf)
        top = jnp.maximum(
            jnp.max(low, axis=0, keepdims=True),
            jnp.max(diag, axis=0, keepdims=True),
        )
        e = jnp.exp2((low - top) * factor)
        f = jnp.exp2((diag - top) * factor)
        inv = 1.0 / (
            jnp.sum(e, axis=0, keepdims=True) + jnp.sum(f, axis=0, keepdims=True)
        )
        p1_ref[:HALF, out] = (e * inv).astype(BF)
        p1_ref[HALF:, out] = (f * inv).astype(BF)


def probs_of(at, queries, keys):
    heads = 2 * PER
    steps = heads // Q_STEP
    per = steps // 2
    wide = Q_STEP * HALF
    return pl.pallas_call(
        _probs_kernel,
        grid_spec=pltpu.PrefetchScalarGridSpec(
            num_scalar_prefetch=1,
            grid=(steps,),
            in_specs=[
                pl.BlockSpec((LEN, Q_STEP * HD), lambda i, o: (0, o[0] + i)),
                pl.BlockSpec((LEN, HD), lambda i, o: (0, o[1] + i // per)),
            ],
            out_specs=[
                pl.BlockSpec((HALF, wide), lambda i, o: (0, i)),
                pl.BlockSpec((LEN, wide), lambda i, o: (0, i)),
                TOKEN,
            ],
        ),
        out_shape=[
            pltpu.HBM((HALF, heads * HALF), BF),
            pltpu.HBM((LEN, heads * HALF), BF),
            jax.ShapeDtypeStruct((1,), jnp.int32),
        ],
        compiler_params=_params(1),
        cost_estimate=pl.CostEstimate(
            flops=heads * 3 * HALF * HALF * HD * 2,
            bytes_accessed=heads * (3 * HALF * HALF + LEN * HD) * 2,
            transcendentals=heads * 3 * HALF * HALF,
        ),
    )(at, queries, keys)


SHARD = 256
P_STEP = 2


def _project_kernel(counts, first, last, where, *refs):
    del where
    xs, refs = refs[: 4 * P_STEP], refs[4 * P_STEP :]
    n = len(counts)
    streams, refs = (refs[:n], refs[n : 2 * n]), refs[2 * n :]
    k = pl.program_id(0)
    if not last:
        refs[-1][0] = 0
        refs = refs[:-1]
    acc = refs[-1]

    @pl.when(k == 0)
    def _():
        acc[...] = jnp.zeros_like(acc) if first else refs[0][...]

    at = 0
    for i, count in enumerate(counts):

        @pl.when((k >= at) & (k < at + count))
        def _():
            deep = jnp.concatenate([streams[0][i][...], streams[1][i][...]], axis=0)
            for s in range(2):
                x = jnp.concatenate(
                    [r[...] for r in xs[s * 2 * P_STEP : (s + 1) * 2 * P_STEP]], axis=1
                )
                acc[s * LEN : (s + 1) * LEN] += jnp.dot(
                    x, deep, preferred_element_type=F32
                )

        at += count

    if last:

        @pl.when(k == at - 1)
        def _():
            for s in range(2):
                refs[-2][:, s * LEN : (s + 1) * LEN] = (
                    acc[s * LEN : (s + 1) * LEN].T.astype(BF)
                )


def project(where, xa, xb, a_pieces, b_pieces, before=None, last=False):
    deep = P_STEP * SHARD
    counts = [p.shape[0] // deep for p in a_pieces]
    n = sum(counts)
    first = before is None
    x_specs = [
        pl.BlockSpec(
            (LEN, SHARD), lambda k, w, c=c, j=j: (0, w[(c * n + k) * P_STEP + j])
        )
        for c in range(2)
        for j in range(P_STEP)
    ] * 2
    w_specs = [
        pl.BlockSpec(
            (deep, 2 * WIDE),
            lambda k, w, a=sum(counts[:i]), c=count: (jnp.clip(k - a, 0, c - 1), 0),
        )
        for i, count in enumerate(counts)
    ] * 2
    whole = pl.BlockSpec((2 * LEN, 2 * WIDE), lambda k, w: (0, 0))

    def kernel(*refs):
        _project_kernel(counts, first, last, *refs)

    return pl.pallas_call(
        kernel,
        grid_spec=pltpu.PrefetchScalarGridSpec(
            num_scalar_prefetch=1,
            grid=(n,),
            in_specs=[*x_specs, *w_specs, *([] if first else [whole])],
            out_specs=pl.BlockSpec((2 * WIDE, 2 * LEN), lambda k, w: (0, 0)) if last else [whole, TOKEN],
            scratch_shapes=[pltpu.VMEM((2 * LEN, 2 * WIDE), F32)] if last else [],
        ),
        out_shape=jax.ShapeDtypeStruct((2 * WIDE, 2 * LEN), BF)
        if last
        else [
            (pltpu.HBM if first else jax.ShapeDtypeStruct)((2 * LEN, 2 * WIDE), F32),
            jax.ShapeDtypeStruct((1,), jnp.int32),
        ],
        compiler_params=_params(1),
        cost_estimate=pl.CostEstimate(
            flops=2 * LEN * deep * 2 * n * 2 * WIDE * 2,
            bytes_accessed=n * deep * (4 * LEN + 4 * WIDE) * 2,
            transcendentals=0,
        ),
    )(
        where,
        *[xa] * (2 * P_STEP),
        *[xb] * (2 * P_STEP),
        *a_pieces,
        *b_pieces,
        *([] if first else [before]),
    )


H_STEP = 4


def _pull_kernel(a0_ref, a1_ref, b0_ref, b1_ref, v_ref, t_ref, o_ref, acc):
    s, h = pl.program_id(0), pl.program_id(2)

    @pl.when(h == 0)
    def _():
        acc[...] = jnp.zeros_like(acc)

    def back(o):
        out, tan = o[:HD], o[HD:]
        square = jnp.sum(out * out, axis=0, keepdims=True) * (1.0 / HD)
        cross = jnp.sum(out * tan, axis=0, keepdims=True) * (1.0 / HD)
        inv2 = 1.0 / (square + EPSILON)
        pull = inv2 * cross * (1.0 + EPSILON * inv2)
        return (inv2 * (tan - out * pull)).astype(BF)

    def go(p0_ref, p1_ref):
        both = jnp.concatenate([v_ref[...], t_ref[...]], axis=0)
        w0 = back(jnp.dot(both[:, :HALF], p0_ref[...], preferred_element_type=F32))
        w1 = back(jnp.dot(both, p1_ref[...], preferred_element_type=F32))
        acc[:HALF] += lax.dot_general(p0_ref[...], w0, NT, preferred_element_type=F32)
        acc[...] += lax.dot_general(p1_ref[...], w1, NT, preferred_element_type=F32)

    @pl.when(s == 0)
    def _():
        go(a0_ref, a1_ref)

    @pl.when(s == 1)
    def _():
        go(b0_ref, b1_ref)

    @pl.when(h == PER // H_STEP - 1)
    def _():
        o_ref[...] = acc[...].T.astype(BF)


def pull_back(a0, a1, b0, b1, projected):
    steps = PER // H_STEP
    wide = H_STEP * HALF

    def in_a(s, g, h):
        return 0, jnp.where(s == 0, g * steps + h, 2 * steps - 1)

    def in_b(s, g, h):
        return 0, s * (g * steps + h)

    return pl.pallas_call(
        _pull_kernel,
        grid=(2, 2, steps),
        in_specs=[
            pl.BlockSpec((HALF, wide), in_a),
            pl.BlockSpec((LEN, wide), in_a),
            pl.BlockSpec((HALF, wide), in_b),
            pl.BlockSpec((LEN, wide), in_b),
            pl.BlockSpec((HD, LEN), lambda s, g, h: (g, s)),
            pl.BlockSpec((HD, LEN), lambda s, g, h: (2 + g, s)),
        ],
        out_specs=pl.BlockSpec((HD, LEN), lambda s, g, h: (g, s)),
        out_shape=jax.ShapeDtypeStruct((WIDE, 2 * LEN), BF),
        scratch_shapes=[pltpu.VMEM((LEN, HD), F32)],
        compiler_params=_params(3),
    )(a0, a1, b0, b1, projected, projected)


G_COLS = 2048
OWN = 128


def _ggn_kernel(pa_ref, pb_ref, xa_ref, xb_ref, o_ref):
    total = jnp.dot(pa_ref[...], xa_ref[...], preferred_element_type=F32)
    total += jnp.dot(pb_ref[...], xb_ref[...], preferred_element_type=F32)
    for j in range(G_COLS // OWN):
        o_ref[j] = total[:, j * OWN : (j + 1) * OWN].astype(BF)


def curvature(pulled, xa, xb):
    depth = xa.shape[1]
    return pl.pallas_call(
        _ggn_kernel,
        grid=(depth // G_COLS,),
        in_specs=[
            pl.BlockSpec((WIDE, LEN), lambda i: (0, 0)),
            pl.BlockSpec((WIDE, LEN), lambda i: (0, 1)),
            pl.BlockSpec((LEN, G_COLS), lambda i: (0, i)),
            pl.BlockSpec((LEN, G_COLS), lambda i: (0, i)),
        ],
        out_specs=pl.BlockSpec((G_COLS // OWN, WIDE, OWN), lambda i: (i, 0, 0)),
        out_shape=pltpu.HBM((depth // OWN, WIDE, OWN), BF),
        compiler_params=_params(1),
    )(pulled, pulled, xa, xb)


ANY = pl.BlockSpec(memory_space=pl.ANY)
WHOLE = pl.BlockSpec(memory_space=pltpu.VMEM)


def narrow(core, value, direction):
    def kernel(core_ref, value_ref, direction_ref, o_ref):
        del core_ref
        o_ref[:, :WIDE] = value_ref[...]
        o_ref[:, WIDE:] = direction_ref[...].astype(BF)

    rows = value.shape[0]
    part = pl.BlockSpec((rows, WIDE), lambda i, c: (0, c[0]))
    return pl.pallas_call(
        kernel,
        grid_spec=pltpu.PrefetchScalarGridSpec(
            num_scalar_prefetch=1,
            grid=(1,),
            in_specs=[part, part],
            out_specs=pl.BlockSpec((rows, 2 * WIDE), lambda i, c: (0, 0)),
        ),
        out_shape=jax.ShapeDtypeStruct((rows, 2 * WIDE), BF),
        compiler_params=_params(1),
    )(core, value, direction)


def chosen(yh, own, swapped, after):
    def kernel(yh_ref, own_ref, swapped_ref, _, low_ref, high_ref):
        @pl.when(yh_ref[0] == 0)
        def _():
            low_ref[...] = own_ref[...]
            high_ref[...] = swapped_ref[...]

        @pl.when(yh_ref[0] != 0)
        def _():
            low_ref[...] = swapped_ref[...]
            high_ref[...] = own_ref[...]

    return pl.pallas_call(
        kernel,
        in_specs=[pl.BlockSpec(memory_space=pltpu.SMEM), WHOLE, WHOLE, ANY],
        out_specs=[WHOLE, WHOLE],
        out_shape=[jax.ShapeDtypeStruct(own.shape, BF)] * 2,
        compiler_params=pltpu.CompilerParams(vmem_limit_bytes=VMEM),
    )(yh, own, swapped, after)


def halves(arrays, after):
    n = len(arrays)
    half = arrays[0].shape[0] // 2
    steps = max(half // 256, 1)
    rows = half // steps

    def kernel(*refs):
        for a, o in zip(refs[:n], refs[-n:]):
            o[...] = a[...]

    shape = (rows, arrays[0].shape[1])
    return pl.pallas_call(
        kernel,
        grid=(steps,),
        in_specs=[
            pl.BlockSpec(shape, lambda i, c=c % 2: (i + c * steps, 0)) for c in range(n)
        ]
        + [TOKEN] * len(after),
        out_specs=[pl.BlockSpec(shape, lambda i: (i, 0))] * n,
        out_shape=[jax.ShapeDtypeStruct((half, shape[1]), BF)] * n,
        compiler_params=_params(1),
    )(*arrays, *after)


def joined(lists, after):
    flat = sum(lists, [])

    def kernel(*refs):
        at = 0
        for arrays, o in zip(lists, refs[-len(lists) :]):
            row = 0
            for _ in arrays:
                n = refs[at].shape[0]
                o[row : row + n] = refs[at][...]
                row, at = row + n, at + 1

    return pl.pallas_call(
        kernel,
        in_specs=[WHOLE] * len(flat) + [TOKEN] * len(after),
        out_specs=[WHOLE] * len(lists),
        out_shape=[
            jax.ShapeDtypeStruct((sum(a.shape[0] for a in l), l[0].shape[1]), BF)
            for l in lists
        ],
        compiler_params=pltpu.CompilerParams(vmem_limit_bytes=VMEM),
    )(*flat, *after)


def for_partner(other, queries, keys, after):
    wide = 2 * PER * HD

    def kernel(other_ref, q_ref, k_ref, _, o_ref):
        del other_ref
        o_ref[:, :wide] = q_ref[...]
        o_ref[:, wide:] = k_ref[...]

    return pl.pallas_call(
        kernel,
        grid_spec=pltpu.PrefetchScalarGridSpec(
            num_scalar_prefetch=1,
            grid=(1,),
            in_specs=[
                pl.BlockSpec((LEN, wide), lambda i, o: (0, o[0])),
                pl.BlockSpec((LEN, WIDE), lambda i, o: (0, o[0])),
                TOKEN,
            ],
            out_specs=pl.BlockSpec((LEN, wide + WIDE), lambda i, o: (0, 0)),
        ),
        out_shape=jax.ShapeDtypeStruct((LEN, wide + WIDE), BF),
        compiler_params=_params(1),
    )(other, queries, keys, after)


def hop(x, axis, by):
    return lax.ppermute(x, axis, [(i, (i + by) % 4) for i in range(4)])


def rings(arrays, axes, after):
    near = [hop(x, a, by) for x, a in zip(arrays, axes) for by in (1, 3)]
    cut = halves(near, after)
    far = [hop(h, axes[i // 2], (1, 3)[i % 2]) for i, h in enumerate(cut)]
    return [(x, *near[2 * i : 2 * i + 2], *far[2 * i : 2 * i + 2]) for i, x in enumerate(arrays)]


S_STEP = 16


def _share_kernel(at_ref, damping_ref, parts_ref, d_ref, r_ref, h_ref, row_ref, acc, *, tokens):
    del at_ref
    i = pl.program_id(0)

    @pl.when(i == 0)
    def _():
        acc[...] = jnp.zeros_like(acc)

    acc[...] += jnp.sum(parts_ref[...].astype(F32), axis=0)

    @pl.when(i == pl.num_programs(0) - 1)
    def _():
        d, r = d_ref[...], r_ref[...]
        h = acc[...].T * (1.0 / tokens) + damping_ref[0] * d
        h_ref[...] = h
        lane = lax.broadcasted_iota(jnp.int32, row_ref.shape, 1)
        row = jnp.zeros(row_ref.shape, F32)
        for j, term in enumerate((r * r, d * h, r * h, h * h)):
            row = jnp.where(lane == j, jnp.sum(term), row)
        row_ref[...] = row


def share(at, damping, parts, direction, residual, devices, tokens):
    n = parts.shape[0] // S_STEP
    own = pl.BlockSpec((OWN, WIDE), lambda i, w: (w[0], w[1]))
    return pl.pallas_call(
        functools.partial(_share_kernel, tokens=tokens),
        grid_spec=pltpu.PrefetchScalarGridSpec(
            num_scalar_prefetch=1,
            grid=(n,),
            in_specs=[
                pl.BlockSpec(memory_space=pltpu.SMEM),
                pl.BlockSpec((S_STEP, WIDE, OWN), lambda i, w: (i, 0, 0)),
                own,
                own,
            ],
            out_specs=[
                pl.BlockSpec((OWN, WIDE), lambda i, w: (0, 0)),
                pl.BlockSpec((devices, 128), lambda i, w: (0, 0)),
            ],
            scratch_shapes=[pltpu.VMEM((WIDE, OWN), F32)],
        ),
        out_shape=[
            jax.ShapeDtypeStruct((OWN, WIDE), F32),
            jax.ShapeDtypeStruct((devices, 128), F32),
        ],
        compiler_params=_params(1),
    )(at, damping, parts, direction, residual)


CHIPS = ("x", "z", "yh", "yl")


def body(normed, queries, keys, value_weight, iterate, residual, direction, damping):
    core, yl = lax.axis_index("c"), lax.axis_index("yl")
    x, z, yh = (lax.axis_index(a) for a in ("x", "z", "yh"))
    other = 1 - core
    swap = [(0, 1), (1, 0)]

    own = narrow(core[None], value_weight, direction)
    normed_b = lax.ppermute(normed, "c", swap)
    swapped = lax.ppermute(own, ("yl", "yh"), Y_SWAP)
    inner = [
        [a, *(hop(a, axis, by) for by in (1, 3, 2))]
        for a, axis in zip(chosen(yh[None], own, swapped, normed_b), "xz")
    ]
    *probs_a, done_a = probs_of(jnp.stack([core * 4, core * 2]), queries, keys)
    lines = joined(inner, [done_a])
    turn = (0, -1, 1, 2)

    def places(steps):
        a_at = [((x + i) % 4) * 8 + (z + s) % 4 * 2 for s in steps for i in turn]
        b_at = [((x + s) % 4) * 8 + (z + i) % 4 * 2 + 1 for s in steps for i in turn]
        return jnp.stack(a_at + b_at).astype(jnp.int32)

    held = pltpu.with_memory_space_constraint(normed, pltpu.HBM)
    some, done_some = project(places((0,)), held, normed_b, lines[:1], lines[1:])
    partner = lax.ppermute(for_partner(other[None], queries, keys, done_some), "c", swap)
    *probs_b, done_b = probs_of(jnp.array([0, 2 * PER], jnp.int32), partner, partner)
    (_, *a, a_far, a_far2), (_, *b, b_far, b_far2) = rings(lines, "zx", [done_b, done_some])
    most, _ = project(places((-1, 1)), held, normed_b, a, b, some)
    projected = project(
        places((2,)), held, normed_b, [a_far, a_far2], [b_far, b_far2], most, True
    )
    pulled = pull_back(*probs_a, *probs_b, projected)
    parts = curvature(pulled, normed, normed_b)
    parts = lax.all_to_all(parts, CHIPS, 0, 0, tiled=True)
    everyone = ("c",) + CHIPS
    devices = lax.axis_size(everyone)
    h, rows = share(
        jnp.stack([yl, core]), damping, parts, direction, residual, devices, devices * normed.shape[0]
    )
    rows = lax.all_to_all(rows, everyone, 0, 0, tiled=True)
    total = jnp.sum(rows, axis=0)
    h_c = lax.ppermute(h, "c", swap)
    h_y = lax.ppermute(h, "yl", swap)
    h_yc = lax.ppermute(h_y, "c", swap)

    def in_order(flag, a, b, axis):
        return jnp.where(
            flag == 0, jnp.concatenate([a, b], axis), jnp.concatenate([b, a], axis)
        )

    hdir = in_order(yl, in_order(core, h, h_c, 1), in_order(core, h_y, h_yc, 1), 0)
    rr, ph, rh, hh = total[0], total[1], total[2], total[3]
    step = rr / ph
    nn = rr - 2.0 * step * rh + step * step * hh
    new_iterate = iterate + step * direction
    new_residual = residual - step * hdir
    new_direction = new_residual + nn / rr * direction
    return (new_iterate, new_residual, new_direction)


def solution(mesh):
    fine = Mesh(
        mesh.devices.reshape(2, 2, 4, 4, 2), ("yl", "c", "x", "z", "yh")
    )
    tokens = P(("yl", "c", "x", "z", "yh"), None)
    rows = P(("x", "z", "yh"), None)
    return jax.shard_map(
        body,
        mesh=fine,
        in_specs=(tokens, tokens, tokens, rows, rows, rows, rows, P()),
        out_specs=(rows, rows, rows),
        check_vma=False,
    )
```
